256 devices in a mesh: dp: 4 (over x), chan: 2 (over z_hi), seq: 32 (over y, z_lo, core).
Axes of the slice: x: 4, y: 4, z: 8 (z_hi: 2, z_lo: 4; z = z_hi * 4 + z_lo), core: 2. Of those that a mesh axis runs over, the one named last changes fastest.
Arguments:
- inputs: bfloat16 [4, 65536, 768], P('dp', 'seq', 'chan'), may hold values from -6 to 6
- gate: bfloat16 [4, 65536, 768], P('dp', 'seq', 'chan'), may hold values from -6 to 6
- cotangent: bfloat16 [4, 65536, 768], P('dp', 'seq', 'chan'), may hold values from -6 to 6
- first_factor: bfloat16 [256, 256, 256], P('seq'), may hold values from -0.375 to 0.375
- second_factor: bfloat16 [256, 256, 256], P('seq'), may hold values from -0.375 to 0.375
Outputs:
- mixed: bfloat16 [4, 65536, 768], P('dp', 'seq', 'chan')
- grad_inputs: bfloat16 [4, 65536, 768], P('dp', 'seq', 'chan')
- grad_first: float32 [256, 256, 256], P('seq', ('dp', 'chan'))
- grad_second: float32 [256, 256, 256], P('seq', ('dp', 'chan'))
The draws below stay inside these ranges and needn't reach their ends.
All inputs are finite; a program needn't handle non-finite values.
Results may differ from the reference program's by a relative error of at most 0.0057.
Values may be sent and summed in bfloat16 or wider, within the bound.
A program may use at most 64 MiB of HBM per device.

```python
import jax
import jax.numpy as jnp
from jax import lax

D = 768
BLK = 256
SEQS = 4
L = 65536


def level_of(rng, dims, split, least, high):
    factor_of, own = 1.0, jax.random.fold_in(rng, 6)
    for dim, shards_of in split:
        heights = jnp.exp(jax.random.uniform(jax.random.fold_in(own, dim), (shards_of,), jnp.float32, least / len(split), high / len(split)))
        factor_of = factor_of * jnp.repeat(heights, dims[dim] // shards_of).reshape([-1 if axis == dim else 1 for axis in range(len(dims))])
    return factor_of


def gaussian(rng, extent, width, most, pieces=(), dtype=jnp.bfloat16):
    drawn = jax.random.normal(rng, extent, jnp.float32) * width
    if len(pieces) > 0:
        drawn = level_of(rng, extent, pieces, -0.22, 0.18) * drawn
    return jnp.clip(drawn, min=-most, max=most).astype(dtype)


def setup_inputs(seed: int = 0) -> dict:
    streams_of = jax.random.split(jax.random.key(seed), 6)
    inputs = gaussian(streams_of[0], (SEQS, L, D), 1.0, 6.0, ((0, 4), (1, 32), (2, 2)))
    gate = gaussian(streams_of[1], (SEQS, L, D), 1.0, 6.0, ((0, 4), (1, 32), (2, 2)))
    cotangent = gaussian(streams_of[2], (SEQS, L, D), 1.0, 6.0, ((0, 4), (1, 32), (2, 2)))
    first_factor = gaussian(streams_of[3], (BLK, BLK, BLK), BLK ** -0.5, 0.375, ((0, 32),))
    second_factor = gaussian(streams_of[4], (BLK, BLK, BLK), BLK ** -0.5, 0.375, ((0, 32),))
    return {"inputs": inputs, "gate": gate, "cotangent": cotangent, "first_factor": first_factor, "second_factor": second_factor}


def reference(inputs, gate, cotangent, first_factor, second_factor):
    first_f = first_factor.astype(jnp.float32)
    second_f = second_factor.astype(jnp.float32)

    def one_sequence(carry, items):
        grad_first, grad_second = carry
        x_seq, g_seq, t_seq = items
        xf = x_seq.reshape(BLK, BLK, D).astype(jnp.float32)
        gf = g_seq.reshape(BLK, BLK, D).astype(jnp.float32)
        tf = t_seq.reshape(BLK, BLK, D).astype(jnp.float32)
        first_mixed = jnp.einsum("ikj,ijc->ikc", first_f, xf).astype(jnp.bfloat16)
        fm = first_mixed.astype(jnp.float32)
        second_mixed = jnp.einsum("kmi,ikc->kmc", second_f, fm)
        mixed = (second_mixed * gf).astype(jnp.bfloat16)
        grad_mixed = (tf * gf).astype(jnp.bfloat16).astype(jnp.float32)
        grad_second = grad_second + jnp.einsum("kmc,ikc->kmi", grad_mixed, fm)
        grad_fm = jnp.einsum("kmi,kmc->ikc", second_f, grad_mixed).astype(jnp.bfloat16).astype(jnp.float32)
        grad_x = jnp.einsum("ikj,ikc->ijc", first_f, grad_fm).astype(jnp.bfloat16)
        grad_first = grad_first + jnp.einsum("ikc,ijc->ikj", grad_fm, xf)
        return (grad_first, grad_second), (mixed.reshape(L, D), grad_x.reshape(L, D))

    zeros = jnp.zeros((BLK, BLK, BLK), jnp.float32)
    (grad_first, grad_second), (mixed, grad_inputs) = lax.scan(one_sequence, (zeros, zeros), (inputs, gate, cotangent))
    return mixed, grad_inputs, grad_first, grad_second
```

```python
import jax
import jax.numpy as jnp
from jax import lax
from jax.experimental import pallas as pl
from jax.experimental.pallas import tpu as pltpu
from jax.sharding import PartitionSpec as P

MESH = pl.DeviceIdType.MESH
F32 = jnp.float32
BF16 = jnp.bfloat16

N = 32
B = 8
K = 256
C = 384
W = C // 128
DP = 4
FCH = 2
FR = 64 // FCH
GCH = 4


def dot(a, b, dims):
    return lax.dot_general(a, b, (dims, ((), ())), preferred_element_type=F32)


def kernel(
    x_h, g_h, t_h, ff_h, sf_h,
    mixed_h, gx_h, gf_h, gs_h,
    x_v, g_v, t_v, ff_v, sf_v, tmp, fs, fr, bs, br, mixed_v, gx_v,
    part2, part1, rs2, rr2, rs1, rr1, cs2, cr2, cs1, cr1, out2, out1,
    in_sem, f_send, f_recv, b_send, b_recv, r_send, r_recv, c_send, c_recv, o_sem,
):
    dp = lax.axis_index("dp")
    ch = lax.axis_index("chan")
    me = lax.axis_index("seq")

    loads = {}
    for i in range(B):
        for n, (h, v) in enumerate(((ff_h, ff_v), (x_h, x_v))):
            loads[n, i] = pltpu.make_async_copy(h.at[i], v.at[i], in_sem.at[n, i])
            loads[n, i].start()
    for i in range(B):
        for n, (h, v) in enumerate(((t_h, t_v), (g_h, g_v), (sf_h, sf_v))):
            loads[n + 2, i] = pltpu.make_async_copy(h.at[i], v.at[i], in_sem.at[n + 2, i])
            loads[n + 2, i].start()

    barrier = pltpu.get_barrier_semaphore()

    def greet(s, carry):
        pl.semaphore_signal(
            barrier, inc=1, device_id={"seq": lax.rem(me + s, N)}, device_id_type=MESH
        )
        return carry

    lax.fori_loop(1, N, greet, 0)
    for s in range(1, DP):
        pl.semaphore_signal(
            barrier, inc=1, device_id={"dp": lax.rem(dp + s, DP)}, device_id_type=MESH
        )
    pl.semaphore_signal(barrier, inc=1, device_id={"chan": 1 - ch}, device_id_type=MESH)

    def exchange(src, dst, c, send_sem, recv_sem):
        def one(s, carry):
            to = lax.rem(me + s, N)
            pltpu.make_async_remote_copy(
                src_ref=src.at[c, to],
                dst_ref=dst.at[c, me],
                send_sem=send_sem.at[c],
                recv_sem=recv_sem.at[c],
                device_id={"seq": to},
                device_id_type=MESH,
            ).start()
            return carry

        lax.fori_loop(1, N, one, 0)
        pltpu.make_async_copy(src.at[c, me], dst.at[c, me], recv_sem.at[c]).start()

    def arrived(dst, sem):
        pltpu.make_async_copy(dst, dst, sem).wait()

    for c in range(FCH):
        for p in range(FR // 16):
            both = []
            for i in (c * (B // FCH) + 2 * p, c * (B // FCH) + 2 * p + 1):
                loads[0, i].wait()
                loads[1, i].wait()
                both.append(dot(ff_v[i], x_v[i], ((1,), (0,))).reshape(N, B, C))
            fs[c, :, 16 * p : 16 * p + 16, :] = jnp.concatenate(both, axis=1).astype(BF16)
        if c == 0:
            pl.semaphore_wait(barrier, N - 1 + DP - 1 + 1)
        exchange(fs, fr, c, f_send, f_recv)

    for k in range(B):
        for n in (2, 3, 4):
            loads[n, k].wait()
        t_v[k] = (t_v[k].astype(F32) * g_v[k].astype(F32)).astype(BF16)
        grad = dot(sf_v[k], t_v[k], ((0,), (0,)))
        for w in range(W):
            tmp[w, pl.ds(k, K, stride=B), :] = grad[:, 128 * w : 128 * w + 128]
    for c in range(GCH):

        def pack(q, carry):
            rows = pl.multiple_of(q * 64 + c * 16, 16)
            for w in range(W):
                bs[c, q, :, 128 * w : 128 * w + 128] = tmp[w, pl.ds(rows, 16), :].astype(BF16)
            return carry

        lax.fori_loop(0, N, pack, 0)
        exchange(bs, br, c, b_send, b_recv)

    def reduce_send(src, dst, n):
        for s in range(1, DP):
            to = lax.rem(dp + s, DP)
            pltpu.make_async_remote_copy(
                src_ref=src.at[to],
                dst_ref=dst.at[s - 1],
                send_sem=r_send.at[n],
                recv_sem=r_recv.at[n],
                device_id={"dp": to},
                device_id_type=MESH,
            ).start()

    def summed(part, recv, half, first, count):
        own = pl.multiple_of(dp * 64 + half * 32, 32)
        rows = pl.multiple_of(half * 32, 32)
        total = part[first : first + count, pl.ds(own, 32), :]
        for s in range(DP - 1):
            total = total + recv[s, :, pl.ds(rows, 32), :].astype(F32)
        return total

    def chan_send(part, recv, send, land, out, n, first, count):
        arrived(recv, r_recv.at[n])
        send[...] = summed(part, recv, 1 - ch, first, count).astype(BF16)
        pltpu.make_async_remote_copy(
            src_ref=send,
            dst_ref=land,
            send_sem=c_send.at[n],
            recv_sem=c_recv.at[n],
            device_id={"chan": 1 - ch},
            device_id_type=MESH,
        ).start()
        out[first : first + count] = summed(part, recv, ch, first, count)

    def chan_done(land, out, n, first, count):
        arrived(land, c_recv.at[n])
        out[first : first + count] = out[first : first + count] + land[...].astype(F32)

    for c in range(FCH):
        arrived(fr.at[c], f_recv.at[c])

        def unpack(q, carry):
            rows = pl.multiple_of(q * 64 + c * FR, FR)
            for w in range(W):
                tmp[w, pl.ds(rows, FR), :] = fr[c, q, :, 128 * w : 128 * w + 128].astype(F32)
            return carry

        lax.fori_loop(0, N, unpack, 0)
    stores = []
    for k in range(B):
        piece = jnp.concatenate(
            [tmp[w, pl.ds(k, K, stride=B), :].astype(BF16) for w in range(W)], axis=1
        )
        mixed_v[k] = (dot(sf_v[k], piece, ((1,), (0,))) * g_v[k].astype(F32)).astype(BF16)
        stores.append(pltpu.make_async_copy(mixed_v.at[k], mixed_h.at[k], o_sem.at[0, k]))
        stores[-1].start()
        grad = dot(t_v[k], piece, ((1,), (1,)))
        part2[k] = grad
        for d in range(DP):
            rs2[d, k] = grad[64 * d : 64 * d + 64].astype(BF16)
    reduce_send(rs2, rr2, GCH)

    for c in range(GCH):
        arrived(br.at[c], b_recv.at[c])
        chunk = br[c].astype(F32)
        for h in range(2):
            i = 2 * c + h
            piece = chunk[:, B * h : B * h + B, :].reshape(K, C).astype(BF16)
            grad = dot(piece, x_v[i], ((1,), (1,)))
            part1[i] = grad
            for d in range(DP):
                rs1[c, d, h] = grad[64 * d : 64 * d + 64].astype(BF16)
        reduce_send(rs1.at[c], rr1.at[c], c)
        for h in range(2):
            i = 2 * c + h
            piece = chunk[:, B * h : B * h + B, :].reshape(K, C).astype(BF16)
            gx_v[i] = dot(ff_v[i], piece, ((0,), (0,))).astype(BF16)
            stores.append(pltpu.make_async_copy(gx_v.at[i], gx_h.at[i], o_sem.at[1, i]))
            stores[-1].start()
        if c == 0:
            chan_send(part2, rr2, cs2, cr2, out2, GCH, 0, B)
        else:
            chan_send(part1, rr1.at[c - 1], cs1.at[c - 1], cr1.at[c - 1], out1, c - 1, 2 * c - 2, 2)
    c = GCH - 1
    chan_done(cr2, out2, GCH, 0, B)
    stores.append(pltpu.make_async_copy(out2, gs_h, o_sem.at[2, 0]))
    stores[-1].start()
    chan_send(part1, rr1.at[c], cs1.at[c], cr1.at[c], out1, c, 2 * c, 2)
    for c in range(GCH):
        chan_done(cr1.at[c], out1, c, 2 * c, 2)
    stores.append(pltpu.make_async_copy(out1, gf_h, o_sem.at[2, 1]))
    stores[-1].start()

    for c in range(FCH):
        sent = fs.at[c, pl.ds(0, N - 1)]
        pltpu.make_async_copy(sent, sent, f_send.at[c]).wait()
    for c in range(GCH):
        sent = bs.at[c, pl.ds(0, N - 1)]
        pltpu.make_async_copy(sent, sent, b_send.at[c]).wait()
        pltpu.make_async_copy(rr1.at[c], rr1.at[c], r_send.at[c]).wait()
        pltpu.make_async_copy(cs1.at[c], cs1.at[c], c_send.at[c]).wait()
    pltpu.make_async_copy(rr2, rr2, r_send.at[GCH]).wait()
    pltpu.make_async_copy(cs2, cs2, c_send.at[GCH]).wait()
    for store in stores:
        store.wait()


def on_device(inputs, gate, cotangent, first_factor, second_factor):
    four = (B, K, C)
    any_spec = pl.BlockSpec(memory_space=pl.ANY)
    vm = pltpu.VMEM
    dma = pltpu.SemaphoreType.DMA
    mixed, gx, gf, gs = pl.pallas_call(
        kernel,
        out_shape=(
            jax.ShapeDtypeStruct(four, BF16),
            jax.ShapeDtypeStruct(four, BF16),
            jax.ShapeDtypeStruct((B, 32, K), F32),
            jax.ShapeDtypeStruct((B, 32, K), F32),
        ),
        in_specs=[any_spec] * 5,
        out_specs=(any_spec,) * 4,
        scratch_shapes=[
            vm(four, BF16), vm(four, BF16), vm(four, BF16), vm((B, K, K), BF16), vm((B, K, K), BF16),
            vm((W, B * K, 128), F32),
            vm((FCH, N, FR, C), BF16), vm((FCH, N, FR, C), BF16),
            vm((GCH, N, 16, C), BF16), vm((GCH, N, 16, C), BF16),
            vm(four, BF16), vm(four, BF16),
            vm((B, K, K), F32), vm((B, K, K), F32),
            vm((DP, B, 64, K), BF16), vm((DP - 1, B, 64, K), BF16),
            vm((GCH, DP, 2, 64, K), BF16), vm((GCH, DP - 1, 2, 64, K), BF16),
            vm((B, 32, K), BF16), vm((B, 32, K), BF16),
            vm((GCH, 2, 32, K), BF16), vm((GCH, 2, 32, K), BF16),
            vm((B, 32, K), F32), vm((B, 32, K), F32),
            dma((5, B)), dma((FCH,)), dma((FCH,)), dma((GCH,)), dma((GCH,)),
            dma((GCH + 1,)), dma((GCH + 1,)), dma((GCH + 1,)), dma((GCH + 1,)), dma((3, B)),
        ],
        compiler_params=pltpu.CompilerParams(
            collective_id=0, has_side_effects=True, vmem_limit_bytes=56 * 2**20
        ),
        cost_estimate=pl.CostEstimate(
            flops=6 * 2 * B * K * K * C, bytes_accessed=10 * 2**20, transcendentals=0
        ),
        name="monarch",
    )(
        inputs.reshape(four), gate.reshape(four), cotangent.reshape(four),
        first_factor, second_factor,
    )
    return mixed.reshape(inputs.shape), gx.reshape(inputs.shape), gf, gs


def solution(mesh):
    rows = P("dp", "seq", "chan")
    factor = P("seq", None, None)
    grad = P("seq", ("dp", "chan"), None)
    return jax.shard_map(
        on_device,
        mesh=mesh,
        in_specs=(rows, rows, rows, factor, factor),
        out_specs=(rows, rows, grad, grad),
        check_vma=False,
    )
```

```python
import jax
import jax.numpy as jnp
from jax import lax
from jax.experimental import pallas as pl
from jax.experimental.pallas import tpu as pltpu
from jax.sharding import PartitionSpec as P

MESH = pl.DeviceIdType.MESH
F32 = jnp.float32
BF16 = jnp.bfloat16

N = 32
B = 8
K = 256
C = 384
W = C // 128
DP = 4
FCH = 4
FR = 64 // FCH
GCH = 4


def dot(a, b, dims):
    return lax.dot_general(a, b, (dims, ((), ())), preferred_element_type=F32)


def kernel(
    x_h, g_h, t_h, ff_h, sf_h,
    mixed_v, gx_v, out1, out2,
    x_v, g_v, t_v, ff_v, sf_v, tmp, fs, fr, bs, br,
    part2, part1, rs2, rr2, rs1, rr1, cs2, cr2, cs1, cr1,
    in_sem, f_send, f_recv, b_send, b_recv, r_send, r_recv, c_send, c_recv,
):
    dp = lax.axis_index("dp")
    ch = lax.axis_index("chan")
    me = lax.axis_index("seq")

    barrier = pltpu.get_barrier_semaphore()

    def greet(s, carry):
        pl.semaphore_signal(
            barrier, inc=1, device_id={"seq": lax.rem(me + s, N)}, device_id_type=MESH
        )
        return carry

    lax.fori_loop(1, N, greet, 0)
    for s in range(1, DP):
        pl.semaphore_signal(
            barrier, inc=1, device_id={"dp": lax.rem(dp + s, DP)}, device_id_type=MESH
        )
    pl.semaphore_signal(barrier, inc=1, device_id={"chan": 1 - ch}, device_id_type=MESH)

    loads = {}
    for i in range(B):
        for n, (h, v) in enumerate(((ff_h, ff_v), (x_h, x_v))):
            loads[n, i] = pltpu.make_async_copy(h.at[i], v.at[i], in_sem.at[n, i])
            loads[n, i].start()
    for i in range(B):
        for n, (h, v) in enumerate(((t_h, t_v), (g_h, g_v), (sf_h, sf_v))):
            loads[n + 2, i] = pltpu.make_async_copy(h.at[i], v.at[i], in_sem.at[n + 2, i])
            loads[n + 2, i].start()

    def exchange(src, dst, c, send_sem, recv_sem):
        def one(s, carry):
            to = lax.rem(me + s, N)
            pltpu.make_async_remote_copy(
                src_ref=src.at[c, to],
                dst_ref=dst.at[c, me],
                send_sem=send_sem.at[c],
                recv_sem=recv_sem.at[c],
                device_id={"seq": to},
                device_id_type=MESH,
            ).start()
            return carry

        lax.fori_loop(1, N, one, 0)
        pltpu.make_async_copy(src.at[c, me], dst.at[c, me], recv_sem.at[c]).start()

    def arrived(dst, sem):
        pltpu.make_async_copy(dst, dst, sem).wait()

    for c in range(FCH):
        for p in range(FR // 16):
            both = []
            for i in (c * (B // FCH) + 2 * p, c * (B // FCH) + 2 * p + 1):
                loads[0, i].wait()
                loads[1, i].wait()
                both.append(dot(ff_v[i], x_v[i], ((1,), (0,))).reshape(N, B, C))
            fs[c, :, 16 * p : 16 * p + 16, :] = jnp.concatenate(both, axis=1).astype(BF16)
        if c == 0:
            pl.semaphore_wait(barrier, N - 1 + DP - 1 + 1)
        exchange(fs, fr, c, f_send, f_recv)

    for k in range(B):
        for n in (2, 3, 4):
            loads[n, k].wait()
        t_v[k] = (t_v[k].astype(F32) * g_v[k].astype(F32)).astype(BF16)
        grad = dot(sf_v[k], t_v[k], ((0,), (0,)))
        for w in range(W):
            tmp[w, pl.ds(k, K, stride=B), :] = grad[:, 128 * w : 128 * w + 128]
    for c in range(GCH):

        def pack(q, carry):
            rows = pl.multiple_of(q * 64 + c * 16, 16)
            for w in range(W):
                bs[c, q, :, 128 * w : 128 * w + 128] = tmp[w, pl.ds(rows, 16), :].astype(BF16)
            return carry

        lax.fori_loop(0, N, pack, 0)
        exchange(bs, br, c, b_send, b_recv)

    def reduce_send(src, dst, n):
        for s in range(1, DP):
            to = lax.rem(dp + s, DP)
            pltpu.make_async_remote_copy(
                src_ref=src.at[to],
                dst_ref=dst.at[s - 1],
                send_sem=r_send.at[n],
                recv_sem=r_recv.at[n],
                device_id={"dp": to},
                device_id_type=MESH,
            ).start()

    def summed(part, recv, half, first, count):
        own = pl.multiple_of(dp * 64 + half * 32, 32)
        rows = pl.multiple_of(half * 32, 32)
        total = part[first : first + count, pl.ds(own, 32), :]
        for s in range(DP - 1):
            total = total + recv[s, :, pl.ds(rows, 32), :].astype(F32)
        return total

    def chan_send(part, recv, send, land, out, n, first, count):
        arrived(recv, r_recv.at[n])
        send[...] = summed(part, recv, 1 - ch, first, count).astype(BF16)
        pltpu.make_async_remote_copy(
            src_ref=send,
            dst_ref=land,
            send_sem=c_send.at[n],
            recv_sem=c_recv.at[n],
            device_id={"chan": 1 - ch},
            device_id_type=MESH,
        ).start()
        out[first : first + count] = summed(part, recv, ch, first, count)

    def chan_done(land, out, n, first, count):
        arrived(land, c_recv.at[n])
        out[first : first + count] = out[first : first + count] + land[...].astype(F32)

    for c in range(FCH):
        arrived(fr.at[c], f_recv.at[c])

        def unpack(q, carry):
            rows = pl.multiple_of(q * 64 + c * FR, FR)
            for w in range(W):
                tmp[w, pl.ds(rows, FR), :] = fr[c, q, :, 128 * w : 128 * w + 128].astype(F32)
            return carry

        lax.fori_loop(0, N, unpack, 0)
    for k in range(B):
        piece = jnp.concatenate(
            [tmp[w, pl.ds(k, K, stride=B), :].astype(BF16) for w in range(W)], axis=1
        )
        mixed_v[k] = (dot(sf_v[k], piece, ((1,), (0,))) * g_v[k].astype(F32)).astype(BF16)
        grad = dot(t_v[k], piece, ((1,), (1,)))
        part2[k] = grad
        for d in range(DP):
            rs2[d, k] = grad[64 * d : 64 * d + 64].astype(BF16)
    reduce_send(rs2, rr2, GCH)

    for c in range(GCH):
        arrived(br.at[c], b_recv.at[c])
        chunk = br[c].astype(F32)
        for h in range(2):
            i = 2 * c + h
            piece = chunk[:, B * h : B * h + B, :].reshape(K, C).astype(BF16)
            grad = dot(piece, x_v[i], ((1,), (1,)))
            part1[i] = grad
            for d in range(DP):
                rs1[c, d, h] = grad[64 * d : 64 * d + 64].astype(BF16)
        reduce_send(rs1.at[c], rr1.at[c], c)
        for h in range(2):
            i = 2 * c + h
            piece = chunk[:, B * h : B * h + B, :].reshape(K, C).astype(BF16)
            gx_v[i] = dot(ff_v[i], piece, ((0,), (0,))).astype(BF16)
        if c == 1:
            chan_send(part2, rr2, cs2, cr2, out2, GCH, 0, B)
        if c > 0:
            chan_send(part1, rr1.at[c - 1], cs1.at[c - 1], cr1.at[c - 1], out1, c - 1, 2 * c - 2, 2)
    c = GCH - 1
    chan_done(cr2, out2, GCH, 0, B)
    chan_send(part1, rr1.at[c], cs1.at[c], cr1.at[c], out1, c, 2 * c, 2)
    for c in range(GCH):
        chan_done(cr1.at[c], out1, c, 2 * c, 2)

    for c in range(FCH):
        sent = fs.at[c, pl.ds(0, N - 1)]
        pltpu.make_async_copy(sent, sent, f_send.at[c]).wait()
    for c in range(GCH):
        sent = bs.at[c, pl.ds(0, N - 1)]
        pltpu.make_async_copy(sent, sent, b_send.at[c]).wait()
        pltpu.make_async_copy(rr1.at[c], rr1.at[c], r_send.at[c]).wait()
        pltpu.make_async_copy(cs1.at[c], cs1.at[c], c_send.at[c]).wait()
    pltpu.make_async_copy(rr2, rr2, r_send.at[GCH]).wait()
    pltpu.make_async_copy(cs2, cs2, c_send.at[GCH]).wait()


def store(mixed_v, gx_v, gf_v, gs_v, mixed_h, gx_h, gf_h, gs_h, sem):
    pairs = ((mixed_v, mixed_h), (gx_v, gx_h), (gf_v, gf_h), (gs_v, gs_h))
    copies = [pltpu.make_async_copy(v, h, sem.at[n]) for n, (v, h) in enumerate(pairs)]
    for copy in copies:
        copy.start()
    for copy in copies:
        copy.wait()


def on_device(inputs, gate, cotangent, first_factor, second_factor):
    four = (B, K, C)
    any_spec = pl.BlockSpec(memory_space=pl.ANY)
    vm = pltpu.VMEM
    dma = pltpu.SemaphoreType.DMA
    shapes = ((four, BF16), (four, BF16), ((B, 32, K), F32), ((B, 32, K), F32))
    results = pl.pallas_call(
        kernel,
        out_shape=(vm(four, BF16), vm(four, BF16), vm((B, 32, K), F32), vm((B, 32, K), F32)),
        in_specs=[any_spec] * 5,
        out_specs=(pl.BlockSpec(memory_space=pltpu.VMEM),) * 4,
        scratch_shapes=[
            vm(four, BF16), vm(four, BF16), vm(four, BF16), vm((B, K, K), BF16), vm((B, K, K), BF16),
            vm((W, B * K, 128), F32),
            vm((FCH, N, FR, C), BF16), vm((FCH, N, FR, C), BF16),
            vm((GCH, N, 16, C), BF16), vm((GCH, N, 16, C), BF16),
            vm((B, K, K), F32), vm((B, K, K), F32),
            vm((DP, B, 64, K), BF16), vm((DP - 1, B, 64, K), BF16),
            vm((GCH, DP, 2, 64, K), BF16), vm((GCH, DP - 1, 2, 64, K), BF16),
            vm((B, 32, K), BF16), vm((B, 32, K), BF16),
            vm((GCH, 2, 32, K), BF16), vm((GCH, 2, 32, K), BF16),
            dma((5, B)), dma((FCH,)), dma((FCH,)), dma((GCH,)), dma((GCH,)),
            dma((GCH + 1,)), dma((GCH + 1,)), dma((GCH + 1,)), dma((GCH + 1,)),
        ],
        compiler_params=pltpu.CompilerParams(
            collective_id=0, has_side_effects=True, vmem_limit_bytes=56 * 2**20
        ),
        cost_estimate=pl.CostEstimate(
            flops=6 * 2 * B * K * K * C, bytes_accessed=10 * 2**20, transcendentals=0
        ),
        name="monarch",
    )(
        inputs.reshape(four), gate.reshape(four), cotangent.reshape(four),
        first_factor, second_factor,
    )
    mixed, gx, gf, gs = pl.pallas_call(
        store,
        out_shape=tuple(jax.ShapeDtypeStruct(*shape) for shape in shapes),
        in_specs=[pl.BlockSpec(memory_space=pltpu.VMEM)] * 4,
        out_specs=(any_spec,) * 4,
        scratch_shapes=[dma((4,))],
        name="store",
        compiler_params=pltpu.CompilerParams(vmem_limit_bytes=2**20),
    )(*results)
    return mixed.reshape(inputs.shape), gx.reshape(inputs.shape), gf, gs


def solution(mesh):
    rows = P("dp", "seq", "chan")
    factor = P("seq", None, None)
    grad = P("seq", ("dp", "chan"), None)
    return jax.shard_map(
        on_device,
        mesh=mesh,
        in_specs=(rows, rows, rows, factor, factor),
        out_specs=(rows, rows, grad, grad),
        check_vma=False,
    )
```

```python
import jax
import jax.numpy as jnp
from jax import lax
from jax.experimental import pallas as pl
from jax.experimental.pallas import tpu as pltpu
from jax.sharding import PartitionSpec as P

MESH = pl.DeviceIdType.MESH
F32 = jnp.float32
BF16 = jnp.bfloat16

N = 32
B = 8
K = 256
C = 384
W = C // 128
DP = 4
FCH = 4
FR = 64 // FCH
GCH = 4


def dot(a, b, dims):
    return lax.dot_general(a, b, (dims, ((), ())), preferred_element_type=F32)


def kernel(
    x_h, g_h, t_h, ff_h, sf_h,
    mixed_v, gx_v, out1, out2,
    x_v, g_v, t_v, ff_v, sf_v, tmp, fs, fr, bs, br,
    part2, part1, rs2, rr2, rs1, rr1, cs2, cr2, cs1, cr1,
    in_sem, f_send, f_recv, b_send, b_recv, r_send, r_recv, c_send, c_recv,
):
    dp = lax.axis_index("dp")
    ch = lax.axis_index("chan")
    me = lax.axis_index("seq")

    barrier = pltpu.get_barrier_semaphore()

    def greet(s, carry):
        pl.semaphore_signal(
            barrier, inc=1, device_id={"seq": lax.rem(me + s, N)}, device_id_type=MESH
        )
        return carry

    lax.fori_loop(1, N, greet, 0)
    for s in range(1, DP):
        pl.semaphore_signal(
            barrier, inc=1, device_id={"dp": lax.rem(dp + s, DP)}, device_id_type=MESH
        )
    pl.semaphore_signal(barrier, inc=1, device_id={"chan": 1 - ch}, device_id_type=MESH)

    loads = {}
    for i in range(B):
        for n, (h, v) in enumerate(((ff_h, ff_v), (x_h, x_v))):
            loads[n, i] = pltpu.make_async_copy(h.at[i], v.at[i], in_sem.at[n, i])
            loads[n, i].start()
    for i in range(B):
        for n, (h, v) in enumerate(((t_h, t_v), (g_h, g_v), (sf_h, sf_v))):
            loads[n + 2, i] = pltpu.make_async_copy(h.at[i], v.at[i], in_sem.at[n + 2, i])
            loads[n + 2, i].start()

    def exchange(src, dst, c, send_sem, recv_sem):
        def one(s, carry):
            to = lax.rem(me + s, N)
            pltpu.make_async_remote_copy(
                src_ref=src.at[c, to],
                dst_ref=dst.at[c, me],
                send_sem=send_sem.at[c],
                recv_sem=recv_sem.at[c],
                device_id={"seq": to},
                device_id_type=MESH,
            ).start()
            return carry

        lax.fori_loop(1, N, one, 0)
        pltpu.make_async_copy(src.at[c, me], dst.at[c, me], recv_sem.at[c]).start()

    def arrived(dst, sem):
        pltpu.make_async_copy(dst, dst, sem).wait()

    for c in range(FCH):
        for p in range(FR // 16):
            both = []
            for i in (c * (B // FCH) + 2 * p, c * (B // FCH) + 2 * p + 1):
                loads[0, i].wait()
                loads[1, i].wait()
                both.append(dot(ff_v[i], x_v[i], ((1,), (0,))).reshape(N, B, C))
            fs[c, :, 16 * p : 16 * p + 16, :] = jnp.concatenate(both, axis=1).astype(BF16)
        if c == 0:
            pl.semaphore_wait(barrier, N - 1 + DP - 1 + 1)
        exchange(fs, fr, c, f_send, f_recv)

    for k in range(B):
        for n in (2, 3, 4):
            loads[n, k].wait()
        t_v[k] = (t_v[k].astype(F32) * g_v[k].astype(F32)).astype(BF16)
        grad = dot(sf_v[k], t_v[k], ((0,), (0,)))
        for w in range(W):
            tmp[w, pl.ds(k, K, stride=B), :] = grad[:, 128 * w : 128 * w + 128]
    for c in range(GCH):

        def pack(q, carry):
            rows = pl.multiple_of(q * 64 + c * 16, 16)
            for w in range(W):
                bs[c, q, :, 128 * w : 128 * w + 128] = tmp[w, pl.ds(rows, 16), :].astype(BF16)
            return carry

        lax.fori_loop(0, N, pack, 0)
        exchange(bs, br, c, b_send, b_recv)

    def reduce_send(src, dst, n):
        for s in range(1, DP):
            to = lax.rem(dp + s, DP)
            pltpu.make_async_remote_copy(
                src_ref=src.at[to],
                dst_ref=dst.at[s - 1],
                send_sem=r_send.at[n],
                recv_sem=r_recv.at[n],
                device_id={"dp": to},
                device_id_type=MESH,
            ).start()

    def summed(part, recv, half, first, count):
        own = pl.multiple_of(dp * 64 + half * 32, 32)
        rows = pl.multiple_of(half * 32, 32)
        total = part[first : first + count, pl.ds(own, 32), :]
        for s in range(DP - 1):
            total = total + recv[s, :, pl.ds(rows, 32), :].astype(F32)
        return total

    def chan_send(part, recv, send, land, out, n, first, count):
        arrived(recv, r_recv.at[n])
        send[...] = summed(part, recv, 1 - ch, first, count).astype(BF16)
        pltpu.make_async_remote_copy(
            src_ref=send,
            dst_ref=land,
            send_sem=c_send.at[n],
            recv_sem=c_recv.at[n],
            device_id={"chan": 1 - ch},
            device_id_type=MESH,
        ).start()
        out[first : first + count] = summed(part, recv, ch, first, count)

    def chan_done(land, out, n, first, count):
        arrived(land, c_recv.at[n])
        out[first : first + count] = out[first : first + count] + land[...].astype(F32)

    for c in range(FCH):
        arrived(fr.at[c], f_recv.at[c])

        def unpack(q, carry):
            rows = pl.multiple_of(q * 64 + c * FR, FR)
            for w in range(W):
                tmp[w, pl.ds(rows, FR), :] = fr[c, q, :, 128 * w : 128 * w + 128].astype(F32)
            return carry

        lax.fori_loop(0, N, unpack, 0)
    for k in range(B):
        piece = jnp.concatenate(
            [tmp[w, pl.ds(k, K, stride=B), :].astype(BF16) for w in range(W)], axis=1
        )
        mixed_v[k] = (dot(sf_v[k], piece, ((1,), (0,))) * g_v[k].astype(F32)).astype(BF16)
        grad = dot(t_v[k], piece, ((1,), (1,)))
        part2[k] = grad
        for d in range(DP):
            rs2[d, k] = grad[64 * d : 64 * d + 64].astype(BF16)
    reduce_send(rs2, rr2, GCH)

    for c in range(GCH):
        arrived(br.at[c], b_recv.at[c])
        chunk = br[c].astype(F32)
        for h in range(2):
            i = 2 * c + h
            piece = chunk[:, B * h : B * h + B, :].reshape(K, C).astype(BF16)
            grad = dot(piece, x_v[i], ((1,), (1,)))
            part1[i] = grad
            for d in range(DP):
                rs1[c, d, h] = grad[64 * d : 64 * d + 64].astype(BF16)
        reduce_send(rs1.at[c], rr1.at[c], c)
        if c == 2:
            chan_send(part2, rr2, cs2, cr2, out2, GCH, 0, B)
        for p in {2: (0, 1), 3: (2,)}.get(c, ()):
            chan_send(part1, rr1.at[p], cs1.at[p], cr1.at[p], out1, p, 2 * p, 2)
    for c in range(GCH):
        chunk = br[c].astype(F32)
        for h in range(2):
            i = 2 * c + h
            piece = chunk[:, B * h : B * h + B, :].reshape(K, C).astype(BF16)
            gx_v[i] = dot(ff_v[i], piece, ((0,), (0,))).astype(BF16)
    c = GCH - 1
    chan_send(part1, rr1.at[c], cs1.at[c], cr1.at[c], out1, c, 2 * c, 2)
    chan_done(cr2, out2, GCH, 0, B)
    for c in range(GCH):
        chan_done(cr1.at[c], out1, c, 2 * c, 2)

    for c in range(FCH):
        sent = fs.at[c, pl.ds(0, N - 1)]
        pltpu.make_async_copy(sent, sent, f_send.at[c]).wait()
    for c in range(GCH):
        sent = bs.at[c, pl.ds(0, N - 1)]
        pltpu.make_async_copy(sent, sent, b_send.at[c]).wait()
        pltpu.make_async_copy(rr1.at[c], rr1.at[c], r_send.at[c]).wait()
        pltpu.make_async_copy(cs1.at[c], cs1.at[c], c_send.at[c]).wait()
    pltpu.make_async_copy(rr2, rr2, r_send.at[GCH]).wait()
    pltpu.make_async_copy(cs2, cs2, c_send.at[GCH]).wait()


def store(mixed_v, gx_v, gf_v, gs_v, mixed_h, gx_h, gf_h, gs_h, sem):
    pairs = ((mixed_v, mixed_h), (gx_v, gx_h), (gf_v, gf_h), (gs_v, gs_h))
    copies = [pltpu.make_async_copy(v, h, sem.at[n]) for n, (v, h) in enumerate(pairs)]
    for copy in copies:
        copy.start()
    for copy in copies:
        copy.wait()


def on_device(inputs, gate, cotangent, first_factor, second_factor):
    four = (B, K, C)
    any_spec = pl.BlockSpec(memory_space=pl.ANY)
    vm = pltpu.VMEM
    dma = pltpu.SemaphoreType.DMA
    shapes = ((four, BF16), (four, BF16), ((B, 32, K), F32), ((B, 32, K), F32))
    results = pl.pallas_call(
        kernel,
        out_shape=(vm(four, BF16), vm(four, BF16), vm((B, 32, K), F32), vm((B, 32, K), F32)),
        in_specs=[any_spec] * 5,
        out_specs=(pl.BlockSpec(memory_space=pltpu.VMEM),) * 4,
        scratch_shapes=[
            vm(four, BF16), vm(four, BF16), vm(four, BF16), vm((B, K, K), BF16), vm((B, K, K), BF16),
            vm((W, B * K, 128), F32),
            vm((FCH, N, FR, C), BF16), vm((FCH, N, FR, C), BF16),
            vm((GCH, N, 16, C), BF16), vm((GCH, N, 16, C), BF16),
            vm((B, K, K), F32), vm((B, K, K), F32),
            vm((DP, B, 64, K), BF16), vm((DP - 1, B, 64, K), BF16),
            vm((GCH, DP, 2, 64, K), BF16), vm((GCH, DP - 1, 2, 64, K), BF16),
            vm((B, 32, K), BF16), vm((B, 32, K), BF16),
            vm((GCH, 2, 32, K), BF16), vm((GCH, 2, 32, K), BF16),
            dma((5, B)), dma((FCH,)), dma((FCH,)), dma((GCH,)), dma((GCH,)),
            dma((GCH + 1,)), dma((GCH + 1,)), dma((GCH + 1,)), dma((GCH + 1,)),
        ],
        compiler_params=pltpu.CompilerParams(
            collective_id=0, has_side_effects=True, vmem_limit_bytes=56 * 2**20
        ),
        cost_estimate=pl.CostEstimate(
            flops=6 * 2 * B * K * K * C, bytes_accessed=10 * 2**20, transcendentals=0
        ),
        name="monarch",
    )(
        inputs.reshape(four), gate.reshape(four), cotangent.reshape(four),
        first_factor, second_factor,
    )
    mixed, gx, gf, gs = pl.pallas_call(
        store,
        out_shape=tuple(jax.ShapeDtypeStruct(*shape) for shape in shapes),
        in_specs=[pl.BlockSpec(memory_space=pltpu.VMEM)] * 4,
        out_specs=(any_spec,) * 4,
        scratch_shapes=[dma((4,))],
        name="store",
        compiler_params=pltpu.CompilerParams(vmem_limit_bytes=2**20),
    )(*results)
    return mixed.reshape(inputs.shape), gx.reshape(inputs.shape), gf, gs


def solution(mesh):
    rows = P("dp", "seq", "chan")
    factor = P("seq", None, None)
    grad = P("seq", ("dp", "chan"), None)
    return jax.shard_map(
        on_device,
        mesh=mesh,
        in_specs=(rows, rows, rows, factor, factor),
        out_specs=(rows, rows, grad, grad),
        check_vma=False,
    )
```
